512 devices in a mesh: dx: 16 (over x, y_lo, core), dy: 32 (over z, y_hi).
Axes of the slice: x: 4, y: 4 (y_hi: 2, y_lo: 2; y = y_hi * 2 + y_lo), z: 16, core: 2. Of those that a mesh axis runs over, the one named last changes fastest.
Arguments:
- image_emb: bfloat16 [131072, 1152], P(('dx', 'dy')), may hold values from -0.19921875 to 0.19921875
- text_feat: bfloat16 [131072, 1152], P(('dx', 'dy')), may hold values from -0.75 to 0.75
- text_head: bfloat16 [1152, 1152], replicated, may hold values from -0.1875 to 0.1875
- log_scale: float32 [1], replicated, may hold values from 1.6 to 2.3
- bias: float32 [1], replicated, may hold values from -3 to -1
Outputs:
- grad_image: float32 [131072, 1152], P(('dx', 'dy'))
- grad_text_feat: float32 [131072, 1152], P(('dx', 'dy'))
- grad_head: float32 [1152, 1152], P('dy', 'dx')
The draws below stay inside these ranges and needn't reach their ends.
All inputs are finite; a program needn't handle non-finite values.
Results may differ from the reference program's by a relative error of at most 0.02.
Values may be sent and summed in bfloat16 or wider, within the bound.
No kernel may reach another device: no remote copies, remote signals or barrier semaphores. Data moves between devices by JAX's collectives and lax.ppermute only.
A program may use at most 64 MiB of HBM per device.

```python
import jax
import jax.numpy as jnp
from jax import lax

E = 1152
W = 1152
ROWS = 256
STEPS = 4
BATCH = 131072
N_DX = 16
N_DY = 32


def raised(result, own_key, source, target, parts, factor):
    owner, partner = [(jnp.arange(result.shape[axis_at]) // (result.shape[axis_at] // parts)).reshape([-1 if axis == axis_at else 1 for axis in range(result.ndim)]) for axis_at in (source, target)]
    chosen = jax.random.permutation(own_key, parts)[partner]
    strong = (owner == chosen) | (owner == (partner + parts // 2) % parts)
    return jnp.where(strong, factor * result, result)


def level_of(stream_key, dims, cuts, least, top_value):
    factor_of = 1.0
    for axis_at, shards_of in cuts:
        steps = jax.random.uniform(jax.random.fold_in(jax.random.fold_in(stream_key, 6), axis_at), (shards_of,), jnp.float32, least / len(cuts), top_value / len(cuts))
        factor_of = factor_of * jnp.repeat(jnp.exp(steps), dims[axis_at] // shards_of).reshape((-1,) + (1,) * (len(dims) - 1 - axis_at))
    return factor_of


def normal_values(stream_key, shape, scale, limit, split=(), kind=jnp.bfloat16):
    drawn = jax.random.normal(stream_key, shape, jnp.float32) * scale
    if len(split) > 0:
        drawn = level_of(stream_key, shape, split, -0.22, 0.18) * drawn
    return jnp.clip(drawn, min=-limit, max=limit).astype(kind)


def heavy_noise(stream_key, dims, spread, bound, shards, heavy, dtype=jnp.bfloat16):
    values = spread * jax.random.normal(stream_key, dims, jnp.float32)
    if shards:
        values = values * level_of(stream_key, dims, shards, -0.22, 0.18)
    return jnp.clip(raised(values, jax.random.fold_in(stream_key, 3), *heavy), -bound, bound).astype(dtype)


def setup_inputs(seed: int = 0) -> dict:
    seeds = jax.random.split(jax.random.key(seed), 6)
    image_emb = normal_values(seeds[0], (BATCH, E), 0.03, 0.19921875, ((0, 512),))
    text_feat = heavy_noise(seeds[1], (BATCH, W), 0.03, 0.75, ((0, 512),), (0, 1, 128, 5.5))
    text_head = normal_values(seeds[2], (W, E), W ** -0.5, 0.1875)
    log_scale = jnp.clip(jax.random.uniform(seeds[3], (1,), jnp.float32, 1.6, 2.3), 1.6, 2.3)
    bias = jnp.clip(jax.random.uniform(seeds[4], (1,), jnp.float32, -3.0, -1.0), -3.0, -1.0)
    return {"image_emb": image_emb, "text_feat": text_feat, "text_head": text_head, "log_scale": log_scale, "bias": bias}


exact_mode = lax.Precision.HIGHEST

def unit_rows(values):
    row_norm = jnp.sqrt(lax.optimization_barrier(jnp.sum(values * values, axis=-1, keepdims=True)) + 1e-06)
    return (values / row_norm, row_norm)

def rounded(values):
    low = lax.optimization_barrier(values.astype(jnp.bfloat16))
    return low.astype(jnp.float32)

def reference(image_emb, text_feat, text_head, log_scale, bias):
    temper = jnp.exp(log_scale[0])
    offset = bias[0]
    head_wide = text_head.astype(jnp.float32)
    diagonal_mask = jnp.arange(ROWS)[:, None] == jnp.arange(ROWS)[None, :]
    sign_diag = jnp.where(diagonal_mask, 1.0, -1.0).astype(jnp.float32)

    def pair_grads(image_blocks, text_blocks, sign_values):
        products = jnp.einsum('qie,qje->qij', image_blocks, text_blocks, precision=exact_mode)
        logits = temper * products + offset
        weight = rounded(-sign_values * jax.nn.sigmoid(-sign_values * logits) * temper)
        image_part = jnp.einsum('qij,qje->qie', weight, text_blocks, precision=exact_mode)
        text_part = jnp.einsum('qij,qie->qje', weight, image_blocks, precision=exact_mode)
        return (image_part, text_part)

    def one_group(pieces):
        image_rows, feat_rows = pieces
        image_unit, image_norm = unit_rows(image_rows.astype(jnp.float32))
        image_low = rounded(image_unit).reshape(N_DY, ROWS, E)
        feat_wide = feat_rows.astype(jnp.float32)
        text_raw = jnp.dot(feat_wide, head_wide, precision=exact_mode)
        text_unit, text_norm = unit_rows(text_raw)
        text_low = rounded(text_unit).reshape(N_DY, ROWS, E)
        image_sum, text_sum = pair_grads(image_low, text_low, sign_diag)
        for distance in range(1, STEPS):
            shifted = jnp.roll(text_low, distance, axis=0)
            image_part, text_part = pair_grads(image_low, shifted, jnp.float32(-1.0))
            image_sum = image_sum + image_part
            text_sum = text_sum + jnp.roll(text_part, -distance, axis=0)
        image_sum = image_sum.reshape(N_DY * ROWS, E)
        text_sum = text_sum.reshape(N_DY * ROWS, E)
        along = lax.optimization_barrier(jnp.sum(image_unit * image_sum, axis=-1, keepdims=True))
        grad_image = (image_sum - image_unit * along) / image_norm
        along_text = lax.optimization_barrier(jnp.sum(text_unit * text_sum, axis=-1, keepdims=True))
        text_back = rounded((text_sum - text_unit * along_text) / text_norm)
        grad_feat = jnp.dot(text_back, head_wide.T, precision=exact_mode)
        head_terms = jnp.einsum('qiw,qie->qwe', feat_wide.reshape(N_DY, ROWS, W), text_back.reshape(N_DY, ROWS, E), precision=exact_mode)
        head_sum = lax.optimization_barrier(jnp.sum(rounded(head_terms), axis=0))
        return (grad_image, grad_feat, head_sum)
    image_groups = image_emb.reshape(N_DX, N_DY * ROWS, E)
    feat_groups = text_feat.reshape(N_DX, N_DY * ROWS, W)
    grad_image, grad_feat, head_sums = lax.map(one_group, (image_groups, feat_groups))
    grad_head = lax.optimization_barrier(jnp.sum(head_sums, axis=0))
    return (grad_image.reshape(N_DX * N_DY * ROWS, E), grad_feat.reshape(N_DX * N_DY * ROWS, W), grad_head)
```

```python
import jax
import jax.numpy as jnp
import numpy as np
from jax import lax
from jax.experimental import pallas as pl
from jax.experimental.pallas import tpu as pltpu
from jax.sharding import PartitionSpec as P

NX, NYL, NC, NZ, NYH = 4, 2, 2, 16, 2
N_DX, N_DY = NX * NYL * NC, NZ * NYH
LANES = 128
VMEM = pl.BlockSpec(memory_space=pltpu.VMEM)
SMEM = pl.BlockSpec(memory_space=pltpu.SMEM)
LIMIT = pltpu.CompilerParams(vmem_limit_bytes=12 << 20)


def unit_rows(values):
    row_norm = jnp.sqrt(jnp.sum(values * values, axis=-1, keepdims=True) + 1e-06)
    return (values / row_norm, row_norm)


def shifted(value, x_steps, dy_steps):
    if x_steps == 0:
        pairs = [(s, (s + dy_steps) % N_DY) for s in range(N_DY)]
        return lax.ppermute(value, "dy", pairs)
    step = NYL * NC
    if dy_steps == 0:
        return lax.ppermute(value, "dx", [(s, (s + step * x_steps) % N_DX) for s in range(N_DX)])
    pairs = [
        (p * N_DY + q, (p + step * x_steps) % N_DX * N_DY + (q + dy_steps) % N_DY)
        for p in range(N_DX)
        for q in range(N_DY)
    ]
    return lax.ppermute(value, ("dx", "dy"), pairs)


def dot_nt(left, right):
    return lax.dot_general(left, right, (((1,), (1,)), ((), ())), preferred_element_type=jnp.float32)


def dot_tn(left, right):
    return lax.dot_general(left, right, (((0,), (0,)), ((), ())), preferred_element_type=jnp.float32)


def dot_nn(left, right):
    return jnp.dot(left, right, preferred_element_type=jnp.float32)


def unit_scaled(values):
    scale = 1.0 / jnp.sqrt(jnp.sum(values * values, axis=-1, keepdims=True) + 1e-06)
    return (values * scale, scale)


def weight_turned(text_low, image_low, sign_values, temper, offset):
    logits = temper * dot_nt(text_low, image_low) + offset
    return (-sign_values * jax.nn.sigmoid(-sign_values * logits) * temper).astype(jnp.bfloat16)


def back_of(text_sum, text_unit, scale):
    along = jnp.sum(text_unit * text_sum, axis=-1, keepdims=True)
    return (text_sum - text_unit * along) * scale


def own_kernel(
    scale_ref,
    feat_ref,
    head_ref,
    image_ref,
    target_ref,
    spread_ref,
    sorted_ref,
    unit_ref,
    scale_col_ref,
    text_low_ref,
    image_low_ref,
    weight_ref,
    first_ref,
):
    rows = feat_ref.shape[0]
    text_unit, scale = unit_scaled(dot_nn(feat_ref[...], head_ref[...]))
    unit_ref[...] = text_unit
    scale_col_ref[...] = scale
    text_low = text_unit.astype(jnp.bfloat16)
    text_low_ref[...] = text_low
    image_low = unit_scaled(image_ref[...].astype(jnp.float32))[0].astype(jnp.bfloat16)
    image_low_ref[...] = image_low
    grid = [lax.broadcasted_iota(jnp.int32, (rows, rows), axis) for axis in range(2)]
    sign_diag = jnp.where(grid[0] == grid[1], 1.0, -1.0)
    weight = weight_turned(text_low, image_low, sign_diag, scale_ref[0], scale_ref[1])
    weight_ref[...] = weight
    first_ref[...] = dot_nn(weight, image_low)
    lane = lax.broadcasted_iota(jnp.int32, spread_ref.shape, 1)
    spread = jnp.where(lane == target_ref[...], 1.0, 0.0).astype(jnp.bfloat16)
    spread_ref[...] = spread
    sorted_ref[...] = dot_nn(feat_ref[...], spread).astype(jnp.bfloat16)


def arrive_kernel(
    core_ref,
    scale_ref,
    visit_ref,
    image_ref,
    head_ref,
    spread_ref,
    image_low_ref,
    text_low_ref,
    unit_ref,
    scale_col_ref,
    first_ref,
    image_far_ref,
    text_next_ref,
    weight_far_ref,
    weight_on_ref,
    weight_fn_ref,
    own_ref,
    part_ref,
    sorted_ref,
    mine_ref,
    other_ref,
    turned_ref,
):
    temper, offset = scale_ref[0], scale_ref[1]
    rows = visit_ref.shape[0]
    image_far = unit_scaled(image_ref[...].astype(jnp.float32))[0].astype(jnp.bfloat16)
    image_far_ref[...] = image_far
    weight_far = weight_turned(text_low_ref[...], image_far, -1.0, temper, offset)
    weight_far_ref[...] = weight_far
    text_own = first_ref[...] + dot_nn(weight_far, image_far)
    own_ref[...] = text_own
    turned_ref[:, :rows] = back_of(text_own, unit_ref[...], scale_col_ref[...]).T

    next_unit, next_scale = unit_scaled(dot_nn(visit_ref[...], head_ref[...]))
    text_next = next_unit.astype(jnp.bfloat16)
    text_next_ref[...] = text_next
    weight_on = weight_turned(text_next, image_low_ref[...], -1.0, temper, offset)
    weight_on_ref[...] = weight_on
    weight_fn = weight_turned(text_next, image_far, -1.0, temper, offset)
    weight_fn_ref[...] = weight_fn
    text_part = dot_nn(weight_on, image_low_ref[...]) + dot_nn(weight_fn, image_far)
    part_ref[...] = text_part.astype(jnp.bfloat16)
    turned_ref[:, rows:] = back_of(text_part, next_unit, next_scale).T
    sorted_ref[...] = dot_nn(visit_ref[...], spread_ref[...]).astype(jnp.bfloat16)

    pieces = NX * NYL
    share = turned_ref.shape[0] // (pieces * NC)
    for out_ref, core in ((mine_ref, core_ref[0]), (other_ref, 1 - core_ref[0])):
        starts = [pl.multiple_of((g * NC + core) * share, 8) for g in range(pieces)]
        cols = [turned_ref[pl.ds(start, share), :] for start in starts]
        out_ref[...] = jnp.concatenate(cols, axis=0).astype(jnp.bfloat16)


def in_vmem(kernel, scalars, arrays, shapes, macs, name, scratch=()):
    return pl.pallas_call(
        kernel,
        in_specs=[SMEM] * len(scalars) + [VMEM] * len(arrays),
        out_specs=[VMEM] * len(shapes),
        out_shape=[jax.ShapeDtypeStruct(*shape) for shape in shapes],
        scratch_shapes=scratch,
        compiler_params=pltpu.CompilerParams(vmem_limit_bytes=12 << 20),
        cost_estimate=pl.CostEstimate(flops=2 * macs, bytes_accessed=8 << 20, transcendentals=0),
        name=name,
    )(*scalars, *arrays)


def in_tiles(block):
    rows, cols = block.shape
    whole, left = cols // LANES, cols % LANES
    high = tail_rows(rows)
    tail = block[:, whole * LANES :]
    blank = jnp.zeros((2 * high - rows, left), block.dtype)
    tail = jnp.concatenate([tail[:high], jnp.concatenate([tail[high:], blank], axis=0)], axis=1)
    tiles = [block[:, t * LANES : (t + 1) * LANES] for t in range(whole)]
    return jnp.concatenate(tiles + [tail], axis=0)


def from_tiles(tiles, rows, cols):
    whole, left = cols // LANES, cols % LANES
    high = tail_rows(rows)
    tail = tiles[whole * rows :]
    tail = jnp.concatenate([tail[:, :left], tail[: rows - high, left : 2 * left]], axis=0)
    parts = [tiles[t * rows : (t + 1) * rows] for t in range(whole)]
    return jnp.concatenate(parts + [tail], axis=1)


def tail_rows(rows):
    return -(-rows // 2 // 8) * 8


def product_kernel(back_ref, feat_ref, visit_ref, *rest):
    out_ref = rest[-1]
    rows = feat_ref.shape[0]
    share = back_ref.shape[0] // (NX * NYL)
    used = back_ref.shape[0] * NC // NYH
    half = feat_ref.shape[1] // NYH
    lanes = pl.ds(pl.multiple_of(pl.program_id(0) * half, LANES), half)
    total = dot_nn(back_ref[:, :rows], feat_ref[:, lanes])
    total += dot_nn(back_ref[:, rows:], visit_ref[:, lanes])
    for part in range(NX * NYL):
        cut = in_tiles(total[part * share : (part + 1) * share, :used])
        if len(rest) > 1:
            cut += rest[0][part, pl.program_id(0)].astype(jnp.float32)
        out_ref[part, 0] = cut.astype(jnp.bfloat16)


def head_product(back, feat, visit, *added):
    cols, rows = back.shape
    width = feat.shape[1]
    parts = NX * NYL
    share, used = cols // parts, cols * NC // NYH
    high = used // LANES * share + tail_rows(share)
    return pl.pallas_call(
        product_kernel,
        grid=(NYH,),
        in_specs=[VMEM] * (3 + len(added)),
        out_specs=pl.BlockSpec((parts, 1, high, LANES), lambda i: (0, i, 0, 0)),
        out_shape=jax.ShapeDtypeStruct((parts, NYH, high, LANES), jnp.bfloat16),
        compiler_params=LIMIT,
        cost_estimate=pl.CostEstimate(flops=2 * cols * rows * width, bytes_accessed=4 << 20, transcendentals=0),
        name="head_product",
    )(back, feat, visit, *added)


def pack_kernel(parts_ref, out_ref):
    slots, high, _ = out_ref.shape
    share, used = 3 * high, 3 * high * N_DX // NYH
    total = from_tiles(jnp.sum(parts_ref[...].astype(jnp.float32), axis=0), share, used)
    wide = total.shape[1] // slots
    blank = jnp.zeros((high, LANES - total.shape[0] // high * wide), jnp.float32)
    for z in range(slots):
        piece = total[:, z * wide : (z + 1) * wide]
        pieces = [piece[g * high : (g + 1) * high] for g in range(total.shape[0] // high)]
        out_ref[z] = jnp.concatenate(pieces + [blank], axis=1).astype(jnp.bfloat16)


def summed_and_packed(parts, share):
    return pl.pallas_call(
        pack_kernel,
        in_specs=[VMEM],
        out_specs=VMEM,
        out_shape=jax.ShapeDtypeStruct((NZ, share // 3, LANES), jnp.bfloat16),
        compiler_params=LIMIT,
        name="sum_x_y",
    )(parts)


def unpack_kernel(parts_ref, out_ref):
    total = jnp.sum(parts_ref[...].astype(jnp.float32), axis=0)
    wide, share = out_ref.shape
    high = total.shape[0]
    pieces = [total[:, g * wide : (g + 1) * wide] for g in range(share // high)]
    piece = jnp.concatenate(pieces, axis=0)
    piece = jnp.concatenate([piece, jnp.zeros((share, LANES - wide), jnp.float32)], axis=1)
    piece = jnp.concatenate([piece, jnp.zeros((LANES - share, LANES), jnp.float32)], axis=0)
    out_ref[...] = piece.T[:wide, :share]


def summed_over_z(parts, wide, share):
    return pl.pallas_call(
        unpack_kernel,
        in_specs=[VMEM],
        out_specs=VMEM,
        out_shape=jax.ShapeDtypeStruct((wide, share), jnp.float32),
        compiler_params=LIMIT,
        name="sum_z",
    )(parts)


def text_back_kernel(own_ref, home_ref, unit_ref, scale_col_ref, out_ref):
    text_sum = own_ref[...] + home_ref[...].astype(jnp.float32)
    out_ref[...] = back_of(text_sum, unit_ref[...], scale_col_ref[...]).astype(jnp.bfloat16)


def grad_image_kernel(own_ref, home_ref, image_ref, out_ref):
    image_sum = own_ref[...] + home_ref[...].astype(jnp.float32)
    image_unit, scale = unit_scaled(image_ref[...].astype(jnp.float32))
    out_ref[...] = back_of(image_sum, image_unit, scale)


def by_rows(kernel, arrays, dtype, flops, name):
    rows, width = arrays[0].shape
    tile = rows // 2
    return pl.pallas_call(
        kernel,
        grid=(rows // tile,),
        in_specs=[pl.BlockSpec((tile, array.shape[1]), lambda i: (i, 0)) for array in arrays],
        out_specs=pl.BlockSpec((tile, width), lambda i: (i, 0)),
        out_shape=jax.ShapeDtypeStruct((rows, width), dtype),
        compiler_params=LIMIT,
        cost_estimate=pl.CostEstimate(flops=flops, bytes_accessed=4 << 20, transcendentals=0),
        name=name,
    )(*arrays)


def local(image_emb, text_feat, text_head, log_scale, bias):
    rows, width = image_emb.shape
    wide = width // N_DY
    share = width // N_DX
    temper = jnp.exp(log_scale[0])
    offset = bias[0]
    scales = jnp.stack([temper, offset])
    core = (lax.axis_index("dx") % NC).astype(jnp.int32).reshape(1)

    low, high = jnp.bfloat16, jnp.float32

    text_visit = shifted(text_feat, 0, 1)
    image_visit = shifted(image_emb, 0, -2)

    half = -(-width // NYH // LANES) * LANES
    place = np.arange(width)
    target = place // wide % NYH * half + place // (wide * NYH) * wide + place % wide
    target = jnp.asarray(target.reshape(width, 1), jnp.int32)
    block, square, column = (rows, width), (rows, rows), (rows, 1)
    sort = (rows, NYH * half)
    own = in_vmem(
        own_kernel,
        [scales],
        [text_feat, text_head, image_emb, target],
        [((width, NYH * half), low), (sort, low), (block, high), (column, high)]
        + [(block, low), (block, low), (square, low), (block, high)],
        rows * width * (width + 2 * rows + NYH * half),
        "own_blocks",
    )
    spread, feat_sorted, text_unit, text_scale, text_low, image_low, weight_own, text_first = own
    out = in_vmem(
        arrive_kernel,
        [core, scales],
        [text_visit, image_visit, text_head, spread, image_low, text_low, text_unit, text_scale, text_first],
        [(block, low), (block, low), (square, low), (square, low), (square, low), (block, high)]
        + [(block, low), (sort, low)]
        + [((width // NC, 2 * rows), low)] * 2,
        rows * width * (width + 6 * rows + NYH * half),
        "arrived",
        [pltpu.VMEM((width, 2 * rows), jnp.float32)],
    )
    image_far, text_next, weight_far, weight_on, weight_fn, text_own, text_part = out[:7]
    visit_sorted, back_mine, back_other = out[7:]

    head_other = head_product(back_other, feat_sorted, visit_sorted)
    head_in = lax.ppermute(head_other, "dx", [(p, p ^ 1) for p in range(N_DX)])
    text_part, _ = lax.optimization_barrier((text_part, head_other))
    text_home = shifted(text_part, 0, -1)
    head_part = head_product(back_mine, feat_sorted, visit_sorted, head_in)
    head_part = head_part.reshape(-1, *head_part.shape[2:])
    groups = [
        [
            ((x * NYL + yl) * NC + c) * N_DY + z * NYH + yh
            for x in range(NX)
            for yl in range(NYL)
            for yh in range(NYH)
        ]
        for c in range(NC)
        for z in range(NZ)
    ]
    late = (weight_own, weight_far, weight_on, weight_fn, text_own, head_part)
    weight_own, weight_far, weight_on, weight_fn, text_own, _ = lax.optimization_barrier(late)
    head_part = lax.all_to_all(head_part, ("dx", "dy"), 0, 0, axis_index_groups=groups, tiled=True)
    head_part = summed_and_packed(head_part, share)

    text_back = by_rows(
        text_back_kernel, [text_own, text_home, text_unit, text_scale], low, 2 * 10**10, "text_back"
    )
    image_part = dot_tn(weight_far, text_low) + dot_tn(weight_fn, text_next)
    image_home = shifted(image_part.astype(jnp.bfloat16), 0, 2)
    image_own = dot_tn(weight_own, text_low) + dot_tn(weight_on, text_next)

    late = (image_own, text_back, image_emb, head_part)
    image_own, text_back, image_emb, head_part = lax.optimization_barrier(late)
    groups = [[z * NYH + yh for z in range(NZ)] for yh in range(NYH)]
    head_part = lax.all_to_all(head_part, "dy", 0, 0, axis_index_groups=groups, tiled=True)
    grad_head = summed_over_z(head_part, wide, share)
    grad_image = by_rows(
        grad_image_kernel, [image_own, image_home, image_emb], high, 8 * rows * width, "grad_image"
    )
    grad_feat = dot_nt(text_back, text_head)
    return (grad_image, grad_feat, grad_head)


def solution(mesh):
    return jax.shard_map(
        local,
        mesh=mesh,
        in_specs=(P(("dx", "dy"), None), P(("dx", "dy"), None), P(), P(), P()),
        out_specs=(P(("dx", "dy"), None), P(("dx", "dy"), None), P("dy", "dx")),
        check_vma=False,
    )
```

```python
import jax
import jax.numpy as jnp
import numpy as np
from jax import lax
from jax.experimental import pallas as pl
from jax.experimental.pallas import tpu as pltpu
from jax.sharding import PartitionSpec as P

NX, NYL, NC, NZ, NYH = 4, 2, 2, 16, 2
N_DX, N_DY = NX * NYL * NC, NZ * NYH
LANES = 128
VMEM = pl.BlockSpec(memory_space=pltpu.VMEM)
SMEM = pl.BlockSpec(memory_space=pltpu.SMEM)
LIMIT = pltpu.CompilerParams(vmem_limit_bytes=12 << 20)


def unit_rows(values):
    row_norm = jnp.sqrt(jnp.sum(values * values, axis=-1, keepdims=True) + 1e-06)
    return (values / row_norm, row_norm)


def shifted(value, x_steps, dy_steps):
    if x_steps == 0:
        pairs = [(s, (s + dy_steps) % N_DY) for s in range(N_DY)]
        return lax.ppermute(value, "dy", pairs)
    step = NYL * NC
    if dy_steps == 0:
        return lax.ppermute(value, "dx", [(s, (s + step * x_steps) % N_DX) for s in range(N_DX)])
    pairs = [
        (p * N_DY + q, (p + step * x_steps) % N_DX * N_DY + (q + dy_steps) % N_DY)
        for p in range(N_DX)
        for q in range(N_DY)
    ]
    return lax.ppermute(value, ("dx", "dy"), pairs)


def dot_nt(left, right):
    return lax.dot_general(left, right, (((1,), (1,)), ((), ())), preferred_element_type=jnp.float32)


def dot_tn(left, right):
    return lax.dot_general(left, right, (((0,), (0,)), ((), ())), preferred_element_type=jnp.float32)


def dot_nn(left, right):
    return jnp.dot(left, right, preferred_element_type=jnp.float32)


def unit_scaled(values):
    scale = 1.0 / jnp.sqrt(jnp.sum(values * values, axis=-1, keepdims=True) + 1e-06)
    return (values * scale, scale)


def weight_turned(text_low, image_low, sign_values, temper, offset):
    logits = temper * dot_nt(text_low, image_low) + offset
    return (-sign_values * jax.nn.sigmoid(-sign_values * logits) * temper).astype(jnp.bfloat16)


def back_of(text_sum, text_unit, scale):
    along = jnp.sum(text_unit * text_sum, axis=-1, keepdims=True)
    return (text_sum - text_unit * along) * scale


def own_kernel(
    scale_ref,
    feat_ref,
    head_ref,
    image_ref,
    target_ref,
    spread_ref,
    sorted_ref,
    unit_ref,
    scale_col_ref,
    text_low_ref,
    image_low_ref,
    weight_ref,
    first_ref,
):
    rows = feat_ref.shape[0]
    text_unit, scale = unit_scaled(dot_nn(feat_ref[...], head_ref[...]))
    unit_ref[...] = text_unit
    scale_col_ref[...] = scale
    text_low = text_unit.astype(jnp.bfloat16)
    text_low_ref[...] = text_low
    image_low = unit_scaled(image_ref[...].astype(jnp.float32))[0].astype(jnp.bfloat16)
    image_low_ref[...] = image_low
    grid = [lax.broadcasted_iota(jnp.int32, (rows, rows), axis) for axis in range(2)]
    sign_diag = jnp.where(grid[0] == grid[1], 1.0, -1.0)
    weight = weight_turned(text_low, image_low, sign_diag, scale_ref[0], scale_ref[1])
    weight_ref[...] = weight
    first_ref[...] = dot_nn(weight, image_low)
    lane = lax.broadcasted_iota(jnp.int32, spread_ref.shape, 1)
    spread = jnp.where(lane == target_ref[...], 1.0, 0.0).astype(jnp.bfloat16)
    spread_ref[...] = spread
    sorted_ref[...] = dot_nn(feat_ref[...], spread).astype(jnp.bfloat16)


def arrive_kernel(
    core_ref,
    scale_ref,
    visit_ref,
    image_ref,
    head_ref,
    spread_ref,
    image_low_ref,
    text_low_ref,
    unit_ref,
    scale_col_ref,
    first_ref,
    image_far_ref,
    text_next_ref,
    weight_far_ref,
    weight_on_ref,
    weight_fn_ref,
    own_ref,
    part_ref,
    sorted_ref,
    mine_ref,
    other_ref,
    turned_ref,
):
    temper, offset = scale_ref[0], scale_ref[1]
    rows = visit_ref.shape[0]
    image_far = unit_scaled(image_ref[...].astype(jnp.float32))[0].astype(jnp.bfloat16)
    image_far_ref[...] = image_far
    weight_far = weight_turned(text_low_ref[...], image_far, -1.0, temper, offset)
    weight_far_ref[...] = weight_far
    text_own = first_ref[...] + dot_nn(weight_far, image_far)
    own_ref[...] = text_own
    turned_ref[:, :rows] = back_of(text_own, unit_ref[...], scale_col_ref[...]).T

    next_unit, next_scale = unit_scaled(dot_nn(visit_ref[...], head_ref[...]))
    text_next = next_unit.astype(jnp.bfloat16)
    text_next_ref[...] = text_next
    weight_on = weight_turned(text_next, image_low_ref[...], -1.0, temper, offset)
    weight_on_ref[...] = weight_on
    weight_fn = weight_turned(text_next, image_far, -1.0, temper, offset)
    weight_fn_ref[...] = weight_fn
    text_part = dot_nn(weight_on, image_low_ref[...]) + dot_nn(weight_fn, image_far)
    part_ref[...] = text_part.astype(jnp.bfloat16)
    turned_ref[:, rows:] = back_of(text_part, next_unit, next_scale).T
    sorted_ref[...] = dot_nn(visit_ref[...], spread_ref[...]).astype(jnp.bfloat16)

    pieces = NX * NYL
    share = turned_ref.shape[0] // (pieces * NC)
    for out_ref, core in ((mine_ref, core_ref[0]), (other_ref, 1 - core_ref[0])):
        starts = [pl.multiple_of((g * NC + core) * share, 8) for g in range(pieces)]
        cols = [turned_ref[pl.ds(start, share), :] for start in starts]
        out_ref[...] = jnp.concatenate(cols, axis=0).astype(jnp.bfloat16)


def in_vmem(kernel, scalars, arrays, shapes, macs, name, scratch=()):
    return pl.pallas_call(
        kernel,
        in_specs=[SMEM] * len(scalars) + [VMEM] * len(arrays),
        out_specs=[VMEM] * len(shapes),
        out_shape=[jax.ShapeDtypeStruct(*shape) for shape in shapes],
        scratch_shapes=scratch,
        compiler_params=pltpu.CompilerParams(vmem_limit_bytes=12 << 20),
        cost_estimate=pl.CostEstimate(flops=2 * macs, bytes_accessed=8 << 20, transcendentals=0),
        name=name,
    )(*scalars, *arrays)


def in_tiles(block):
    rows, cols = block.shape
    whole, left = cols // LANES, cols % LANES
    high = tail_rows(rows)
    tail = block[:, whole * LANES :]
    blank = jnp.zeros((2 * high - rows, left), block.dtype)
    tail = jnp.concatenate([tail[:high], jnp.concatenate([tail[high:], blank], axis=0)], axis=1)
    tiles = [block[:, t * LANES : (t + 1) * LANES] for t in range(whole)]
    return jnp.concatenate(tiles + [tail], axis=0)


def from_tiles(tiles, rows, cols):
    whole, left = cols // LANES, cols % LANES
    high = tail_rows(rows)
    tail = tiles[whole * rows :]
    tail = jnp.concatenate([tail[:, :left], tail[: rows - high, left : 2 * left]], axis=0)
    parts = [tiles[t * rows : (t + 1) * rows] for t in range(whole)]
    return jnp.concatenate(parts + [tail], axis=1)


def tail_rows(rows):
    return -(-rows // 2 // 8) * 8


def product_kernel(back_ref, feat_ref, visit_ref, *rest):
    out_ref = rest[-1]
    rows = feat_ref.shape[0]
    share = back_ref.shape[0] // (NX * NYL)
    used = back_ref.shape[0] * NC // NYH
    half = feat_ref.shape[1] // NYH
    for yh in range(NYH):
        lanes = slice(yh * half, (yh + 1) * half)
        total = dot_nn(back_ref[:, :rows], feat_ref[:, lanes])
        total += dot_nn(back_ref[:, rows:], visit_ref[:, lanes])
        for part in range(NX * NYL):
            peer = (part // NYL * NYH + yh) * NYL + part % NYL
            cut = in_tiles(total[part * share : (part + 1) * share, :used])
            if len(rest) > 1:
                cut += rest[0][peer].astype(jnp.float32)
            out_ref[peer] = cut.astype(jnp.bfloat16)


def head_product(back, feat, visit, *added):
    cols, rows = back.shape
    width = feat.shape[1]
    parts = NX * NYL
    share, used = cols // parts, cols * NC // NYH
    shape = (parts * NYH, used // LANES * share + tail_rows(share), LANES)
    return pl.pallas_call(
        product_kernel,
        in_specs=[VMEM] * (3 + len(added)),
        out_specs=VMEM,
        out_shape=jax.ShapeDtypeStruct(shape, jnp.bfloat16),
        compiler_params=LIMIT,
        cost_estimate=pl.CostEstimate(flops=2 * cols * rows * width, bytes_accessed=4 << 20, transcendentals=0),
        name="head_product",
    )(back, feat, visit, *added)


def pack_kernel(parts_ref, out_ref):
    slots, high, _ = out_ref.shape
    share, used = 3 * high, 3 * high * N_DX // NYH
    total = from_tiles(jnp.sum(parts_ref[...].astype(jnp.float32), axis=0), share, used)
    wide = total.shape[1] // slots
    blank = jnp.zeros((high, LANES - total.shape[0] // high * wide), jnp.float32)
    for z in range(slots):
        piece = total[:, z * wide : (z + 1) * wide]
        pieces = [piece[g * high : (g + 1) * high] for g in range(total.shape[0] // high)]
        out_ref[z] = jnp.concatenate(pieces + [blank], axis=1).astype(jnp.bfloat16)


def summed_and_packed(parts, share):
    return pl.pallas_call(
        pack_kernel,
        in_specs=[VMEM],
        out_specs=VMEM,
        out_shape=jax.ShapeDtypeStruct((NZ, share // 3, LANES), jnp.bfloat16),
        compiler_params=LIMIT,
        name="sum_x_y",
    )(parts)


def unpack_kernel(parts_ref, out_ref):
    total = jnp.sum(parts_ref[...].astype(jnp.float32), axis=0)
    wide, share = out_ref.shape
    high = total.shape[0]
    pieces = [total[:, g * wide : (g + 1) * wide] for g in range(share // high)]
    piece = jnp.concatenate(pieces, axis=0)
    piece = jnp.concatenate([piece, jnp.zeros((share, LANES - wide), jnp.float32)], axis=1)
    piece = jnp.concatenate([piece, jnp.zeros((LANES - share, LANES), jnp.float32)], axis=0)
    out_ref[...] = piece.T[:wide, :share]


def summed_over_z(parts, wide, share):
    return pl.pallas_call(
        unpack_kernel,
        in_specs=[VMEM],
        out_specs=VMEM,
        out_shape=jax.ShapeDtypeStruct((wide, share), jnp.float32),
        compiler_params=LIMIT,
        name="sum_z",
    )(parts)


def text_back_kernel(own_ref, home_ref, unit_ref, scale_col_ref, out_ref):
    text_sum = own_ref[...] + home_ref[...].astype(jnp.float32)
    out_ref[...] = back_of(text_sum, unit_ref[...], scale_col_ref[...]).astype(jnp.bfloat16)


def grad_image_kernel(own_ref, home_ref, image_ref, out_ref):
    image_sum = own_ref[...] + home_ref[...].astype(jnp.float32)
    image_unit, scale = unit_scaled(image_ref[...].astype(jnp.float32))
    out_ref[...] = back_of(image_sum, image_unit, scale)


def by_rows(kernel, arrays, dtype, flops, name):
    rows, width = arrays[0].shape
    tile = rows // 2
    return pl.pallas_call(
        kernel,
        grid=(rows // tile,),
        in_specs=[pl.BlockSpec((tile, array.shape[1]), lambda i: (i, 0)) for array in arrays],
        out_specs=pl.BlockSpec((tile, width), lambda i: (i, 0)),
        out_shape=jax.ShapeDtypeStruct((rows, width), dtype),
        compiler_params=LIMIT,
        cost_estimate=pl.CostEstimate(flops=flops, bytes_accessed=4 << 20, transcendentals=0),
        name=name,
    )(*arrays)


def local(image_emb, text_feat, text_head, log_scale, bias):
    rows, width = image_emb.shape
    wide = width // N_DY
    share = width // N_DX
    temper = jnp.exp(log_scale[0])
    offset = bias[0]
    scales = jnp.stack([temper, offset])
    core = (lax.axis_index("dx") % NC).astype(jnp.int32).reshape(1)

    low, high = jnp.bfloat16, jnp.float32

    text_visit = shifted(text_feat, 0, 1)
    image_visit = shifted(image_emb, 0, -2)

    half = -(-width // NYH // LANES) * LANES
    place = np.arange(width)
    target = place // wide % NYH * half + place // (wide * NYH) * wide + place % wide
    target = jnp.asarray(target.reshape(width, 1), jnp.int32)
    block, square, column = (rows, width), (rows, rows), (rows, 1)
    sort = (rows, NYH * half)
    own = in_vmem(
        own_kernel,
        [scales],
        [text_feat, text_head, image_emb, target],
        [((width, NYH * half), low), (sort, low), (block, high), (column, high)]
        + [(block, low), (block, low), (square, low), (block, high)],
        rows * width * (width + 2 * rows + NYH * half),
        "own_blocks",
    )
    spread, feat_sorted, text_unit, text_scale, text_low, image_low, weight_own, text_first = own
    out = in_vmem(
        arrive_kernel,
        [core, scales],
        [text_visit, image_visit, text_head, spread, image_low, text_low, text_unit, text_scale, text_first],
        [(block, low), (block, low), (square, low), (square, low), (square, low), (block, high)]
        + [(block, low), (sort, low)]
        + [((width // NC, 2 * rows), low)] * 2,
        rows * width * (width + 6 * rows + NYH * half),
        "arrived",
        [pltpu.VMEM((width, 2 * rows), jnp.float32)],
    )
    image_far, text_next, weight_far, weight_on, weight_fn, text_own, text_part = out[:7]
    visit_sorted, back_mine, back_other = out[7:]

    head_other = head_product(back_other, feat_sorted, visit_sorted)
    head_in = lax.ppermute(head_other, "dx", [(p, p ^ 1) for p in range(N_DX)])
    text_part, _ = lax.optimization_barrier((text_part, head_other))
    text_home = shifted(text_part, 0, -1)
    head_part = head_product(back_mine, feat_sorted, visit_sorted, head_in)
    groups = [
        [
            ((x * NYL + yl) * NC + c) * N_DY + z * NYH + yh
            for x in range(NX)
            for yh in range(NYH)
            for yl in range(NYL)
        ]
        for c in range(NC)
        for z in range(NZ)
    ]
    late = (weight_own, weight_far, weight_on, weight_fn, text_own, head_part)
    weight_own, weight_far, weight_on, weight_fn, text_own, _ = lax.optimization_barrier(late)
    head_part = lax.all_to_all(head_part, ("dx", "dy"), 0, 0, axis_index_groups=groups, tiled=True)
    head_part = summed_and_packed(head_part, share)

    text_back = by_rows(
        text_back_kernel, [text_own, text_home, text_unit, text_scale], low, 2 * 10**10, "text_back"
    )
    image_part = dot_tn(weight_far, text_low) + dot_tn(weight_fn, text_next)
    image_home = shifted(image_part.astype(jnp.bfloat16), 0, 2)
    image_own = dot_tn(weight_own, text_low) + dot_tn(weight_on, text_next)

    late = (image_own, text_back, image_emb, head_part)
    image_own, text_back, image_emb, head_part = lax.optimization_barrier(late)
    groups = [[z * NYH + yh for z in range(NZ)] for yh in range(NYH)]
    head_part = lax.all_to_all(head_part, "dy", 0, 0, axis_index_groups=groups, tiled=True)
    grad_head = summed_over_z(head_part, wide, share)
    grad_image = by_rows(
        grad_image_kernel, [image_own, image_home, image_emb], high, 8 * rows * width, "grad_image"
    )
    grad_feat = dot_nt(text_back, text_head)
    return (grad_image, grad_feat, grad_head)


def solution(mesh):
    return jax.shard_map(
        local,
        mesh=mesh,
        in_specs=(P(("dx", "dy"), None), P(("dx", "dy"), None), P(), P(), P()),
        out_specs=(P(("dx", "dy"), None), P(("dx", "dy"), None), P("dy", "dx")),
        check_vma=False,
    )
```

```python
import jax
import jax.numpy as jnp
import numpy as np
from jax import lax
from jax.experimental import pallas as pl
from jax.experimental.pallas import tpu as pltpu
from jax.sharding import PartitionSpec as P

NX, NYL, NC, NZ, NYH = 4, 2, 2, 16, 2
N_DX, N_DY = NX * NYL * NC, NZ * NYH
LANES = 128
VMEM = pl.BlockSpec(memory_space=pltpu.VMEM)
SMEM = pl.BlockSpec(memory_space=pltpu.SMEM)
LIMIT = pltpu.CompilerParams(vmem_limit_bytes=12 << 20)


def unit_rows(values):
    row_norm = jnp.sqrt(jnp.sum(values * values, axis=-1, keepdims=True) + 1e-06)
    return (values / row_norm, row_norm)


def shifted(value, x_steps, dy_steps):
    if x_steps == 0:
        pairs = [(s, (s + dy_steps) % N_DY) for s in range(N_DY)]
        return lax.ppermute(value, "dy", pairs)
    step = NYL * NC
    if dy_steps == 0:
        return lax.ppermute(value, "dx", [(s, (s + step * x_steps) % N_DX) for s in range(N_DX)])
    pairs = [
        (p * N_DY + q, (p + step * x_steps) % N_DX * N_DY + (q + dy_steps) % N_DY)
        for p in range(N_DX)
        for q in range(N_DY)
    ]
    return lax.ppermute(value, ("dx", "dy"), pairs)


def dot_nt(left, right):
    return lax.dot_general(left, right, (((1,), (1,)), ((), ())), preferred_element_type=jnp.float32)


def dot_tn(left, right):
    return lax.dot_general(left, right, (((0,), (0,)), ((), ())), preferred_element_type=jnp.float32)


def dot_nn(left, right):
    return jnp.dot(left, right, preferred_element_type=jnp.float32)


def unit_scaled(values):
    scale = 1.0 / jnp.sqrt(jnp.sum(values * values, axis=-1, keepdims=True) + 1e-06)
    return (values * scale, scale)


def weight_turned(text_low, image_low, sign_values, temper, offset):
    logits = temper * dot_nt(text_low, image_low) + offset
    return (-sign_values * jax.nn.sigmoid(-sign_values * logits) * temper).astype(jnp.bfloat16)


def back_of(text_sum, text_unit, scale):
    along = jnp.sum(text_unit * text_sum, axis=-1, keepdims=True)
    return (text_sum - text_unit * along) * scale


def own_kernel(
    scale_ref,
    feat_ref,
    head_ref,
    image_ref,
    target_ref,
    spread_ref,
    sorted_ref,
    unit_ref,
    scale_col_ref,
    text_low_ref,
    image_low_ref,
    weight_ref,
    first_ref,
):
    rows = feat_ref.shape[0]
    text_unit, scale = unit_scaled(dot_nn(feat_ref[...], head_ref[...]))
    unit_ref[...] = text_unit
    scale_col_ref[...] = scale
    text_low = text_unit.astype(jnp.bfloat16)
    text_low_ref[...] = text_low
    image_low = unit_scaled(image_ref[...].astype(jnp.float32))[0].astype(jnp.bfloat16)
    image_low_ref[...] = image_low
    grid = [lax.broadcasted_iota(jnp.int32, (rows, rows), axis) for axis in range(2)]
    sign_diag = jnp.where(grid[0] == grid[1], 1.0, -1.0)
    weight = weight_turned(text_low, image_low, sign_diag, scale_ref[0], scale_ref[1])
    weight_ref[...] = weight
    first_ref[...] = dot_nn(weight, image_low)
    lane = lax.broadcasted_iota(jnp.int32, spread_ref.shape, 1)
    spread = jnp.where(lane == target_ref[...], 1.0, 0.0).astype(jnp.bfloat16)
    spread_ref[...] = spread
    sorted_ref[...] = dot_nn(feat_ref[...], spread).astype(jnp.bfloat16)


def arrive_kernel(
    core_ref,
    scale_ref,
    visit_ref,
    image_ref,
    head_ref,
    spread_ref,
    image_low_ref,
    text_low_ref,
    unit_ref,
    scale_col_ref,
    first_ref,
    image_far_ref,
    text_next_ref,
    weight_far_ref,
    weight_on_ref,
    weight_fn_ref,
    own_ref,
    part_ref,
    sorted_ref,
    mine_ref,
    other_ref,
    turned_ref,
):
    temper, offset = scale_ref[0], scale_ref[1]
    rows = visit_ref.shape[0]
    image_far = unit_scaled(image_ref[...].astype(jnp.float32))[0].astype(jnp.bfloat16)
    image_far_ref[...] = image_far
    weight_far = weight_turned(text_low_ref[...], image_far, -1.0, temper, offset)
    weight_far_ref[...] = weight_far
    text_own = first_ref[...] + dot_nn(weight_far, image_far)
    own_ref[...] = text_own
    turned_ref[:, :rows] = back_of(text_own, unit_ref[...], scale_col_ref[...]).T

    next_unit, next_scale = unit_scaled(dot_nn(visit_ref[...], head_ref[...]))
    text_next = next_unit.astype(jnp.bfloat16)
    text_next_ref[...] = text_next
    weight_on = weight_turned(text_next, image_low_ref[...], -1.0, temper, offset)
    weight_on_ref[...] = weight_on
    weight_fn = weight_turned(text_next, image_far, -1.0, temper, offset)
    weight_fn_ref[...] = weight_fn
    text_part = dot_nn(weight_on, image_low_ref[...]) + dot_nn(weight_fn, image_far)
    part_ref[...] = text_part.astype(jnp.bfloat16)
    turned_ref[:, rows:] = back_of(text_part, next_unit, next_scale).T
    sorted_ref[...] = dot_nn(visit_ref[...], spread_ref[...]).astype(jnp.bfloat16)

    pieces = NX * NYL
    share = turned_ref.shape[0] // (pieces * NC)
    for out_ref, core in ((mine_ref, core_ref[0]), (other_ref, 1 - core_ref[0])):
        starts = [pl.multiple_of((g * NC + core) * share, 8) for g in range(pieces)]
        cols = [turned_ref[pl.ds(start, share), :] for start in starts]
        out_ref[...] = jnp.concatenate(cols, axis=0).astype(jnp.bfloat16)


def in_vmem(kernel, scalars, arrays, shapes, macs, name, scratch=()):
    return pl.pallas_call(
        kernel,
        in_specs=[SMEM] * len(scalars) + [VMEM] * len(arrays),
        out_specs=[VMEM] * len(shapes),
        out_shape=[jax.ShapeDtypeStruct(*shape) for shape in shapes],
        scratch_shapes=scratch,
        compiler_params=pltpu.CompilerParams(vmem_limit_bytes=12 << 20),
        cost_estimate=pl.CostEstimate(flops=2 * macs, bytes_accessed=8 << 20, transcendentals=0),
        name=name,
    )(*scalars, *arrays)


def in_tiles(block):
    rows, cols = block.shape
    whole, left = cols // LANES, cols % LANES
    high = tail_rows(rows)
    tail = block[:, whole * LANES :]
    blank = jnp.zeros((2 * high - rows, left), block.dtype)
    tail = jnp.concatenate([tail[:high], jnp.concatenate([tail[high:], blank], axis=0)], axis=1)
    tiles = [block[:, t * LANES : (t + 1) * LANES] for t in range(whole)]
    return jnp.concatenate(tiles + [tail], axis=0)


def from_tiles(tiles, rows, cols):
    whole, left = cols // LANES, cols % LANES
    high = tail_rows(rows)
    tail = tiles[whole * rows :]
    tail = jnp.concatenate([tail[:, :left], tail[: rows - high, left : 2 * left]], axis=0)
    parts = [tiles[t * rows : (t + 1) * rows] for t in range(whole)]
    return jnp.concatenate(parts + [tail], axis=1)


def tail_rows(rows):
    return -(-rows // 2 // 8) * 8


def product_kernel(back_ref, feat_ref, visit_ref, *rest):
    out_ref = rest[-1]
    rows = feat_ref.shape[0]
    share = back_ref.shape[0] // (NX * NYL)
    used = back_ref.shape[0] * NC // NYH
    half = feat_ref.shape[1] // NYH
    for yh in range(NYH):
        lanes = slice(yh * half, (yh + 1) * half)
        total = dot_nn(back_ref[:, :rows], feat_ref[:, lanes])
        total += dot_nn(back_ref[:, rows:], visit_ref[:, lanes])
        for part in range(NX * NYL):
            peer = (yh * NYL + part % NYL) * NX + part // NYL
            cut = in_tiles(total[part * share : (part + 1) * share, :used])
            if len(rest) > 1:
                cut += rest[0][peer].astype(jnp.float32)
            out_ref[peer] = cut.astype(jnp.bfloat16)


def head_product(back, feat, visit, *added):
    cols, rows = back.shape
    width = feat.shape[1]
    parts = NX * NYL
    share, used = cols // parts, cols * NC // NYH
    shape = (parts * NYH, used // LANES * share + tail_rows(share), LANES)
    return pl.pallas_call(
        product_kernel,
        in_specs=[VMEM] * (3 + len(added)),
        out_specs=VMEM,
        out_shape=jax.ShapeDtypeStruct(shape, jnp.bfloat16),
        compiler_params=LIMIT,
        cost_estimate=pl.CostEstimate(flops=2 * cols * rows * width, bytes_accessed=4 << 20, transcendentals=0),
        name="head_product",
    )(back, feat, visit, *added)


def pack_kernel(parts_ref, out_ref):
    slots, high, _ = out_ref.shape
    share, used = 3 * high, 3 * high * N_DX // NYH
    total = from_tiles(jnp.sum(parts_ref[...].astype(jnp.float32), axis=0), share, used)
    wide = total.shape[1] // slots
    blank = jnp.zeros((high, LANES - total.shape[0] // high * wide), jnp.float32)
    for z in range(slots):
        piece = total[:, z * wide : (z + 1) * wide]
        pieces = [piece[g * high : (g + 1) * high] for g in range(total.shape[0] // high)]
        out_ref[z] = jnp.concatenate(pieces + [blank], axis=1).astype(jnp.bfloat16)


def summed_and_packed(parts, share):
    return pl.pallas_call(
        pack_kernel,
        in_specs=[VMEM],
        out_specs=VMEM,
        out_shape=jax.ShapeDtypeStruct((NZ, share // 3, LANES), jnp.bfloat16),
        compiler_params=LIMIT,
        name="sum_x_y",
    )(parts)


def unpack_kernel(parts_ref, out_ref):
    total = jnp.sum(parts_ref[...].astype(jnp.float32), axis=0)
    wide, share = out_ref.shape
    high = total.shape[0]
    pieces = [total[:, g * wide : (g + 1) * wide] for g in range(share // high)]
    piece = jnp.concatenate(pieces, axis=0)
    piece = jnp.concatenate([piece, jnp.zeros((share, LANES - wide), jnp.float32)], axis=1)
    piece = jnp.concatenate([piece, jnp.zeros((LANES - share, LANES), jnp.float32)], axis=0)
    out_ref[...] = piece.T[:wide, :share]


def summed_over_z(parts, wide, share):
    return pl.pallas_call(
        unpack_kernel,
        in_specs=[VMEM],
        out_specs=VMEM,
        out_shape=jax.ShapeDtypeStruct((wide, share), jnp.float32),
        compiler_params=LIMIT,
        name="sum_z",
    )(parts)


def text_back_kernel(own_ref, home_ref, unit_ref, scale_col_ref, out_ref):
    text_sum = own_ref[...] + home_ref[...].astype(jnp.float32)
    out_ref[...] = back_of(text_sum, unit_ref[...], scale_col_ref[...]).astype(jnp.bfloat16)


def grad_image_kernel(own_ref, home_ref, image_ref, out_ref):
    image_sum = own_ref[...] + home_ref[...].astype(jnp.float32)
    image_unit, scale = unit_scaled(image_ref[...].astype(jnp.float32))
    out_ref[...] = back_of(image_sum, image_unit, scale)


def by_rows(kernel, arrays, dtype, flops, name):
    rows, width = arrays[0].shape
    tile = rows // 2
    return pl.pallas_call(
        kernel,
        grid=(rows // tile,),
        in_specs=[pl.BlockSpec((tile, array.shape[1]), lambda i: (i, 0)) for array in arrays],
        out_specs=pl.BlockSpec((tile, width), lambda i: (i, 0)),
        out_shape=jax.ShapeDtypeStruct((rows, width), dtype),
        compiler_params=LIMIT,
        cost_estimate=pl.CostEstimate(flops=flops, bytes_accessed=4 << 20, transcendentals=0),
        name=name,
    )(*arrays)


def local(image_emb, text_feat, text_head, log_scale, bias):
    rows, width = image_emb.shape
    wide = width // N_DY
    share = width // N_DX
    temper = jnp.exp(log_scale[0])
    offset = bias[0]
    scales = jnp.stack([temper, offset])
    core = (lax.axis_index("dx") % NC).astype(jnp.int32).reshape(1)

    low, high = jnp.bfloat16, jnp.float32

    text_visit = shifted(text_feat, 0, 1)
    image_visit = shifted(image_emb, 0, -2)

    half = -(-width // NYH // LANES) * LANES
    place = np.arange(width)
    target = place // wide % NYH * half + place // (wide * NYH) * wide + place % wide
    target = jnp.asarray(target.reshape(width, 1), jnp.int32)
    block, square, column = (rows, width), (rows, rows), (rows, 1)
    sort = (rows, NYH * half)
    own = in_vmem(
        own_kernel,
        [scales],
        [text_feat, text_head, image_emb, target],
        [((width, NYH * half), low), (sort, low), (block, high), (column, high)]
        + [(block, low), (block, low), (square, low), (block, high)],
        rows * width * (width + 2 * rows + NYH * half),
        "own_blocks",
    )
    spread, feat_sorted, text_unit, text_scale, text_low, image_low, weight_own, text_first = own
    out = in_vmem(
        arrive_kernel,
        [core, scales],
        [text_visit, image_visit, text_head, spread, image_low, text_low, text_unit, text_scale, text_first],
        [(block, low), (block, low), (square, low), (square, low), (square, low), (block, high)]
        + [(block, low), (sort, low)]
        + [((width // NC, 2 * rows), low)] * 2,
        rows * width * (width + 6 * rows + NYH * half),
        "arrived",
        [pltpu.VMEM((width, 2 * rows), jnp.float32)],
    )
    image_far, text_next, weight_far, weight_on, weight_fn, text_own, text_part = out[:7]
    visit_sorted, back_mine, back_other = out[7:]

    head_other = head_product(back_other, feat_sorted, visit_sorted)
    head_in = lax.ppermute(head_other, "dx", [(p, p ^ 1) for p in range(N_DX)])
    text_part, _ = lax.optimization_barrier((text_part, head_other))
    text_home = shifted(text_part, 0, -1)
    head_part = head_product(back_mine, feat_sorted, visit_sorted, head_in)
    groups = [
        [
            ((x * NYL + yl) * NC + c) * N_DY + z * NYH + yh
            for yh in range(NYH)
            for yl in range(NYL)
            for x in range(NX)
        ]
        for c in range(NC)
        for z in range(NZ)
    ]
    late = (weight_own, weight_far, weight_on, weight_fn, text_own, head_part)
    weight_own, weight_far, weight_on, weight_fn, text_own, _ = lax.optimization_barrier(late)
    head_part = lax.all_to_all(head_part, ("dx", "dy"), 0, 0, axis_index_groups=groups, tiled=True)
    head_part = summed_and_packed(head_part, share)

    text_back = by_rows(
        text_back_kernel, [text_own, text_home, text_unit, text_scale], low, 2 * 10**10, "text_back"
    )
    image_part = dot_tn(weight_far, text_low) + dot_tn(weight_fn, text_next)
    image_home = shifted(image_part.astype(jnp.bfloat16), 0, 2)
    image_own = dot_tn(weight_own, text_low) + dot_tn(weight_on, text_next)

    late = (image_own, text_back, image_emb, head_part)
    image_own, text_back, image_emb, head_part = lax.optimization_barrier(late)
    groups = [[z * NYH + yh for z in range(NZ)] for yh in range(NYH)]
    head_part = lax.all_to_all(head_part, "dy", 0, 0, axis_index_groups=groups, tiled=True)
    grad_head = summed_over_z(head_part, wide, share)
    grad_image = by_rows(
        grad_image_kernel, [image_own, image_home, image_emb], high, 8 * rows * width, "grad_image"
    )
    grad_feat = dot_nt(text_back, text_head)
    return (grad_image, grad_feat, grad_head)


def solution(mesh):
    return jax.shard_map(
        local,
        mesh=mesh,
        in_specs=(P(("dx", "dy"), None), P(("dx", "dy"), None), P(), P(), P()),
        out_specs=(P(("dx", "dy"), None), P(("dx", "dy"), None), P("dy", "dx")),
        check_vma=False,
    )
```

```python
import jax
import jax.numpy as jnp
import numpy as np
from jax import lax
from jax.experimental import pallas as pl
from jax.experimental.pallas import tpu as pltpu
from jax.sharding import PartitionSpec as P

NX, NYL, NC, NZ, NYH = 4, 2, 2, 16, 2
N_DX, N_DY = NX * NYL * NC, NZ * NYH
LANES = 128
VMEM = pl.BlockSpec(memory_space=pltpu.VMEM)
SMEM = pl.BlockSpec(memory_space=pltpu.SMEM)
LIMIT = pltpu.CompilerParams(vmem_limit_bytes=12 << 20)


def unit_rows(values):
    row_norm = jnp.sqrt(jnp.sum(values * values, axis=-1, keepdims=True) + 1e-06)
    return (values / row_norm, row_norm)


def shifted(value, x_steps, dy_steps):
    if x_steps == 0:
        pairs = [(s, (s + dy_steps) % N_DY) for s in range(N_DY)]
        return lax.ppermute(value, "dy", pairs)
    step = NYL * NC
    if dy_steps == 0:
        return lax.ppermute(value, "dx", [(s, (s + step * x_steps) % N_DX) for s in range(N_DX)])
    pairs = [
        (p * N_DY + q, (p + step * x_steps) % N_DX * N_DY + (q + dy_steps) % N_DY)
        for p in range(N_DX)
        for q in range(N_DY)
    ]
    return lax.ppermute(value, ("dx", "dy"), pairs)


def dot_nt(left, right):
    return lax.dot_general(left, right, (((1,), (1,)), ((), ())), preferred_element_type=jnp.float32)


def dot_tn(left, right):
    return lax.dot_general(left, right, (((0,), (0,)), ((), ())), preferred_element_type=jnp.float32)


def dot_nn(left, right):
    return jnp.dot(left, right, preferred_element_type=jnp.float32)


def unit_scaled(values):
    scale = 1.0 / jnp.sqrt(jnp.sum(values * values, axis=-1, keepdims=True) + 1e-06)
    return (values * scale, scale)


def weight_turned(text_low, image_low, sign_values, temper, offset):
    logits = temper * dot_nt(text_low, image_low) + offset
    return (-sign_values * jax.nn.sigmoid(-sign_values * logits) * temper).astype(jnp.bfloat16)


def back_of(text_sum, text_unit, scale):
    along = jnp.sum(text_unit * text_sum, axis=-1, keepdims=True)
    return (text_sum - text_unit * along) * scale


def own_kernel(
    scale_ref,
    feat_ref,
    head_ref,
    image_ref,
    target_ref,
    spread_ref,
    sorted_ref,
    unit_ref,
    scale_col_ref,
    text_low_ref,
    image_low_ref,
    weight_ref,
    first_ref,
):
    rows = feat_ref.shape[0]
    text_unit, scale = unit_scaled(dot_nn(feat_ref[...], head_ref[...]))
    unit_ref[...] = text_unit
    scale_col_ref[...] = scale
    text_low = text_unit.astype(jnp.bfloat16)
    text_low_ref[...] = text_low
    image_low = unit_scaled(image_ref[...].astype(jnp.float32))[0].astype(jnp.bfloat16)
    image_low_ref[...] = image_low
    grid = [lax.broadcasted_iota(jnp.int32, (rows, rows), axis) for axis in range(2)]
    sign_diag = jnp.where(grid[0] == grid[1], 1.0, -1.0)
    weight = weight_turned(text_low, image_low, sign_diag, scale_ref[0], scale_ref[1])
    weight_ref[...] = weight
    first_ref[...] = dot_nn(weight, image_low)
    lane = lax.broadcasted_iota(jnp.int32, spread_ref.shape, 1)
    spread = jnp.where(lane == target_ref[...], 1.0, 0.0).astype(jnp.bfloat16)
    spread_ref[...] = spread
    sorted_ref[...] = dot_nn(feat_ref[...], spread).astype(jnp.bfloat16)


def arrive_kernel(
    core_ref,
    scale_ref,
    visit_ref,
    image_ref,
    head_ref,
    spread_ref,
    image_low_ref,
    text_low_ref,
    unit_ref,
    scale_col_ref,
    first_ref,
    image_far_ref,
    text_next_ref,
    weight_far_ref,
    weight_on_ref,
    weight_fn_ref,
    own_ref,
    part_ref,
    sorted_ref,
    mine_ref,
    other_ref,
    turned_ref,
):
    temper, offset = scale_ref[0], scale_ref[1]
    rows = visit_ref.shape[0]
    image_far = unit_scaled(image_ref[...].astype(jnp.float32))[0].astype(jnp.bfloat16)
    image_far_ref[...] = image_far
    weight_far = weight_turned(text_low_ref[...], image_far, -1.0, temper, offset)
    weight_far_ref[...] = weight_far
    text_own = first_ref[...] + dot_nn(weight_far, image_far)
    own_ref[...] = text_own
    turned_ref[:, :rows] = back_of(text_own, unit_ref[...], scale_col_ref[...]).T

    next_unit, next_scale = unit_scaled(dot_nn(visit_ref[...], head_ref[...]))
    text_next = next_unit.astype(jnp.bfloat16)
    text_next_ref[...] = text_next
    weight_on = weight_turned(text_next, image_low_ref[...], -1.0, temper, offset)
    weight_on_ref[...] = weight_on
    weight_fn = weight_turned(text_next, image_far, -1.0, temper, offset)
    weight_fn_ref[...] = weight_fn
    text_part = dot_nn(weight_on, image_low_ref[...]) + dot_nn(weight_fn, image_far)
    part_ref[...] = text_part.astype(jnp.bfloat16)
    turned_ref[:, rows:] = back_of(text_part, next_unit, next_scale).T
    sorted_ref[...] = dot_nn(visit_ref[...], spread_ref[...]).astype(jnp.bfloat16)

    pieces = NX * NYL
    share = turned_ref.shape[0] // (pieces * NC)
    for out_ref, core in ((mine_ref, core_ref[0]), (other_ref, 1 - core_ref[0])):
        starts = [pl.multiple_of((g * NC + core) * share, 8) for g in range(pieces)]
        cols = [turned_ref[pl.ds(start, share), :] for start in starts]
        out_ref[...] = jnp.concatenate(cols, axis=0).astype(jnp.bfloat16)


def in_vmem(kernel, scalars, arrays, shapes, macs, name, scratch=()):
    return pl.pallas_call(
        kernel,
        in_specs=[SMEM] * len(scalars) + [VMEM] * len(arrays),
        out_specs=[VMEM] * len(shapes),
        out_shape=[jax.ShapeDtypeStruct(*shape) for shape in shapes],
        scratch_shapes=scratch,
        compiler_params=pltpu.CompilerParams(vmem_limit_bytes=12 << 20),
        cost_estimate=pl.CostEstimate(flops=2 * macs, bytes_accessed=8 << 20, transcendentals=0),
        name=name,
    )(*scalars, *arrays)


def in_tiles(block):
    rows, cols = block.shape
    whole, left = cols // LANES, cols % LANES
    high = tail_rows(rows)
    tail = block[:, whole * LANES :]
    blank = jnp.zeros((2 * high - rows, left), block.dtype)
    tail = jnp.concatenate([tail[:high], jnp.concatenate([tail[high:], blank], axis=0)], axis=1)
    tiles = [block[:, t * LANES : (t + 1) * LANES] for t in range(whole)]
    return jnp.concatenate(tiles + [tail], axis=0)


def from_tiles(tiles, rows, cols):
    whole, left = cols // LANES, cols % LANES
    high = tail_rows(rows)
    tail = tiles[whole * rows :]
    tail = jnp.concatenate([tail[:, :left], tail[: rows - high, left : 2 * left]], axis=0)
    parts = [tiles[t * rows : (t + 1) * rows] for t in range(whole)]
    return jnp.concatenate(parts + [tail], axis=1)


def tail_rows(rows):
    return -(-rows // 2 // 8) * 8


def product_kernel(back_ref, feat_ref, visit_ref, *rest):
    out_ref = rest[-1]
    rows = feat_ref.shape[0]
    share = back_ref.shape[0] // (NX * NYL)
    used = back_ref.shape[0] * NC // NYH
    half = feat_ref.shape[1] // NYH
    for yh in range(NYH):
        lanes = slice(yh * half, (yh + 1) * half)
        total = dot_nn(back_ref[:, :rows], feat_ref[:, lanes])
        total += dot_nn(back_ref[:, rows:], visit_ref[:, lanes])
        for part in range(NX * NYL):
            x = part // NYL
            peer = x * NYL * NYH + (yh * NYL + part % NYL - x) % (NYL * NYH)
            cut = in_tiles(total[part * share : (part + 1) * share, :used])
            if len(rest) > 1:
                cut += rest[0][peer].astype(jnp.float32)
            out_ref[peer] = cut.astype(jnp.bfloat16)


def head_product(back, feat, visit, *added):
    cols, rows = back.shape
    width = feat.shape[1]
    parts = NX * NYL
    share, used = cols // parts, cols * NC // NYH
    shape = (parts * NYH, used // LANES * share + tail_rows(share), LANES)
    return pl.pallas_call(
        product_kernel,
        in_specs=[VMEM] * (3 + len(added)),
        out_specs=VMEM,
        out_shape=jax.ShapeDtypeStruct(shape, jnp.bfloat16),
        compiler_params=LIMIT,
        cost_estimate=pl.CostEstimate(flops=2 * cols * rows * width, bytes_accessed=4 << 20, transcendentals=0),
        name="head_product",
    )(back, feat, visit, *added)


def pack_kernel(parts_ref, out_ref):
    slots, high, _ = out_ref.shape
    share, used = 3 * high, 3 * high * N_DX // NYH
    total = from_tiles(jnp.sum(parts_ref[...].astype(jnp.float32), axis=0), share, used)
    wide = total.shape[1] // slots
    blank = jnp.zeros((high, LANES - total.shape[0] // high * wide), jnp.float32)
    for z in range(slots):
        piece = total[:, z * wide : (z + 1) * wide]
        pieces = [piece[g * high : (g + 1) * high] for g in range(total.shape[0] // high)]
        out_ref[z] = jnp.concatenate(pieces + [blank], axis=1).astype(jnp.bfloat16)


def summed_and_packed(parts, share):
    return pl.pallas_call(
        pack_kernel,
        in_specs=[VMEM],
        out_specs=VMEM,
        out_shape=jax.ShapeDtypeStruct((NZ, share // 3, LANES), jnp.bfloat16),
        compiler_params=LIMIT,
        name="sum_x_y",
    )(parts)


def unpack_kernel(parts_ref, out_ref):
    total = jnp.sum(parts_ref[...].astype(jnp.float32), axis=0)
    wide, share = out_ref.shape
    high = total.shape[0]
    pieces = [total[:, g * wide : (g + 1) * wide] for g in range(share // high)]
    piece = jnp.concatenate(pieces, axis=0)
    piece = jnp.concatenate([piece, jnp.zeros((share, LANES - wide), jnp.float32)], axis=1)
    piece = jnp.concatenate([piece, jnp.zeros((LANES - share, LANES), jnp.float32)], axis=0)
    out_ref[...] = piece.T[:wide, :share]


def summed_over_z(parts, wide, share):
    return pl.pallas_call(
        unpack_kernel,
        in_specs=[VMEM],
        out_specs=VMEM,
        out_shape=jax.ShapeDtypeStruct((wide, share), jnp.float32),
        compiler_params=LIMIT,
        name="sum_z",
    )(parts)


def text_back_kernel(own_ref, home_ref, unit_ref, scale_col_ref, out_ref):
    text_sum = own_ref[...] + home_ref[...].astype(jnp.float32)
    out_ref[...] = back_of(text_sum, unit_ref[...], scale_col_ref[...]).astype(jnp.bfloat16)


def grad_image_kernel(own_ref, home_ref, image_ref, out_ref):
    image_sum = own_ref[...] + home_ref[...].astype(jnp.float32)
    image_unit, scale = unit_scaled(image_ref[...].astype(jnp.float32))
    out_ref[...] = back_of(image_sum, image_unit, scale)


def by_rows(kernel, arrays, dtype, flops, name):
    rows, width = arrays[0].shape
    tile = rows // 2
    return pl.pallas_call(
        kernel,
        grid=(rows // tile,),
        in_specs=[pl.BlockSpec((tile, array.shape[1]), lambda i: (i, 0)) for array in arrays],
        out_specs=pl.BlockSpec((tile, width), lambda i: (i, 0)),
        out_shape=jax.ShapeDtypeStruct((rows, width), dtype),
        compiler_params=LIMIT,
        cost_estimate=pl.CostEstimate(flops=flops, bytes_accessed=4 << 20, transcendentals=0),
        name=name,
    )(*arrays)


def local(image_emb, text_feat, text_head, log_scale, bias):
    rows, width = image_emb.shape
    wide = width // N_DY
    share = width // N_DX
    temper = jnp.exp(log_scale[0])
    offset = bias[0]
    scales = jnp.stack([temper, offset])
    core = (lax.axis_index("dx") % NC).astype(jnp.int32).reshape(1)

    low, high = jnp.bfloat16, jnp.float32

    text_visit = shifted(text_feat, 0, 1)
    image_visit = shifted(image_emb, 0, -2)

    half = -(-width // NYH // LANES) * LANES
    place = np.arange(width)
    target = place // wide % NYH * half + place // (wide * NYH) * wide + place % wide
    target = jnp.asarray(target.reshape(width, 1), jnp.int32)
    block, square, column = (rows, width), (rows, rows), (rows, 1)
    sort = (rows, NYH * half)
    own = in_vmem(
        own_kernel,
        [scales],
        [text_feat, text_head, image_emb, target],
        [((width, NYH * half), low), (sort, low), (block, high), (column, high)]
        + [(block, low), (block, low), (square, low), (block, high)],
        rows * width * (width + 2 * rows + NYH * half),
        "own_blocks",
    )
    spread, feat_sorted, text_unit, text_scale, text_low, image_low, weight_own, text_first = own
    out = in_vmem(
        arrive_kernel,
        [core, scales],
        [text_visit, image_visit, text_head, spread, image_low, text_low, text_unit, text_scale, text_first],
        [(block, low), (block, low), (square, low), (square, low), (square, low), (block, high)]
        + [(block, low), (sort, low)]
        + [((width // NC, 2 * rows), low)] * 2,
        rows * width * (width + 6 * rows + NYH * half),
        "arrived",
        [pltpu.VMEM((width, 2 * rows), jnp.float32)],
    )
    image_far, text_next, weight_far, weight_on, weight_fn, text_own, text_part = out[:7]
    visit_sorted, back_mine, back_other = out[7:]

    head_other = head_product(back_other, feat_sorted, visit_sorted)
    head_in = lax.ppermute(head_other, "dx", [(p, p ^ 1) for p in range(N_DX)])
    text_part, _ = lax.optimization_barrier((text_part, head_other))
    text_home = shifted(text_part, 0, -1)
    head_part = head_product(back_mine, feat_sorted, visit_sorted, head_in)
    groups = [
        [
            ((x * NYL + y % NYL) * NC + c) * N_DY + z * NYH + y // NYL
            for x in range(NX)
            for y in [(x + j) % (NYL * NYH) for j in range(NYL * NYH)]
        ]
        for c in range(NC)
        for z in range(NZ)
    ]
    late = (weight_own, weight_far, weight_on, weight_fn, text_own, head_part)
    weight_own, weight_far, weight_on, weight_fn, text_own, _ = lax.optimization_barrier(late)
    head_part = lax.all_to_all(head_part, ("dx", "dy"), 0, 0, axis_index_groups=groups, tiled=True)
    head_part = summed_and_packed(head_part, share)

    text_back = by_rows(
        text_back_kernel, [text_own, text_home, text_unit, text_scale], low, 2 * 10**10, "text_back"
    )
    image_part = dot_tn(weight_far, text_low) + dot_tn(weight_fn, text_next)
    image_home = shifted(image_part.astype(jnp.bfloat16), 0, 2)
    image_own = dot_tn(weight_own, text_low) + dot_tn(weight_on, text_next)

    late = (image_own, text_back, image_emb, head_part)
    image_own, text_back, image_emb, head_part = lax.optimization_barrier(late)
    groups = [[z * NYH + yh for z in range(NZ)] for yh in range(NYH)]
    head_part = lax.all_to_all(head_part, "dy", 0, 0, axis_index_groups=groups, tiled=True)
    grad_head = summed_over_z(head_part, wide, share)
    grad_image = by_rows(
        grad_image_kernel, [image_own, image_home, image_emb], high, 8 * rows * width, "grad_image"
    )
    grad_feat = dot_nt(text_back, text_head)
    return (grad_image, grad_feat, grad_head)


def solution(mesh):
    return jax.shard_map(
        local,
        mesh=mesh,
        in_specs=(P(("dx", "dy"), None), P(("dx", "dy"), None), P(), P(), P()),
        out_specs=(P(("dx", "dy"), None), P(("dx", "dy"), None), P("dy", "dx")),
        check_vma=False,
    )
```

```python
import jax
import jax.numpy as jnp
import numpy as np
from jax import lax
from jax.experimental import pallas as pl
from jax.experimental.pallas import tpu as pltpu
from jax.sharding import PartitionSpec as P

NX, NYL, NC, NZ, NYH = 4, 2, 2, 16, 2
N_DX, N_DY = NX * NYL * NC, NZ * NYH
LANES = 128
VMEM = pl.BlockSpec(memory_space=pltpu.VMEM)
SMEM = pl.BlockSpec(memory_space=pltpu.SMEM)
LIMIT = pltpu.CompilerParams(vmem_limit_bytes=12 << 20)


def unit_rows(values):
    row_norm = jnp.sqrt(jnp.sum(values * values, axis=-1, keepdims=True) + 1e-06)
    return (values / row_norm, row_norm)


def shifted(value, *dy_steps):
    pairs = [
        (p * N_DY + q, p * N_DY + (q + dy_steps[p % NC]) % N_DY) for p in range(N_DX) for q in range(N_DY)
    ]
    return lax.ppermute(value, ("dx", "dy"), pairs)


def dot_nt(left, right):
    return lax.dot_general(left, right, (((1,), (1,)), ((), ())), preferred_element_type=jnp.float32)


def dot_tn(left, right):
    return lax.dot_general(left, right, (((0,), (0,)), ((), ())), preferred_element_type=jnp.float32)


def dot_nn(left, right):
    return jnp.dot(left, right, preferred_element_type=jnp.float32)


def unit_scaled(values):
    scale = 1.0 / jnp.sqrt(jnp.sum(values * values, axis=-1, keepdims=True) + 1e-06)
    return (values * scale, scale)


def weight_turned(text_low, image_low, sign_values, temper, offset):
    logits = temper * dot_nt(text_low, image_low) + offset
    return (-sign_values * jax.nn.sigmoid(-sign_values * logits) * temper).astype(jnp.bfloat16)


def back_of(text_sum, text_unit, scale):
    along = jnp.sum(text_unit * text_sum, axis=-1, keepdims=True)
    return (text_sum - text_unit * along) * scale


def own_kernel(
    scale_ref,
    feat_ref,
    head_ref,
    image_ref,
    target_ref,
    spread_ref,
    sorted_ref,
    unit_ref,
    scale_col_ref,
    text_low_ref,
    image_low_ref,
    weight_ref,
    first_ref,
):
    rows = feat_ref.shape[0]
    text_unit, scale = unit_scaled(dot_nn(feat_ref[...], head_ref[...]))
    unit_ref[...] = text_unit
    scale_col_ref[...] = scale
    text_low = text_unit.astype(jnp.bfloat16)
    text_low_ref[...] = text_low
    image_low = unit_scaled(image_ref[...].astype(jnp.float32))[0].astype(jnp.bfloat16)
    image_low_ref[...] = image_low
    grid = [lax.broadcasted_iota(jnp.int32, (rows, rows), axis) for axis in range(2)]
    sign_diag = jnp.where(grid[0] == grid[1], 1.0, -1.0)
    weight = weight_turned(text_low, image_low, sign_diag, scale_ref[0], scale_ref[1])
    weight_ref[...] = weight
    first_ref[...] = dot_nn(weight, image_low)
    lane = lax.broadcasted_iota(jnp.int32, spread_ref.shape, 1)
    spread = jnp.where(lane == target_ref[...], 1.0, 0.0).astype(jnp.bfloat16)
    spread_ref[...] = spread
    sorted_ref[...] = dot_nn(feat_ref[...], spread).astype(jnp.bfloat16)


def arrive_kernel(
    core_ref,
    scale_ref,
    early_ref,
    late_ref,
    head_ref,
    spread_ref,
    image_low_ref,
    text_low_ref,
    unit_ref,
    scale_col_ref,
    first_ref,
    image_far_ref,
    text_next_ref,
    weight_far_ref,
    weight_on_ref,
    weight_fn_ref,
    own_ref,
    part_ref,
    sorted_ref,
    mine_ref,
    other_ref,
    turned_ref,
):
    temper, offset = scale_ref[0], scale_ref[1]
    rows = early_ref.shape[0]
    text_early = core_ref[0] == 0
    visit = jnp.where(text_early, early_ref[...], late_ref[...])
    image = jnp.where(text_early, late_ref[...], early_ref[...])
    image_far = unit_scaled(image.astype(jnp.float32))[0].astype(jnp.bfloat16)
    image_far_ref[...] = image_far
    weight_far = weight_turned(text_low_ref[...], image_far, -1.0, temper, offset)
    weight_far_ref[...] = weight_far
    text_own = first_ref[...] + dot_nn(weight_far, image_far)
    own_ref[...] = text_own
    turned_ref[:, :rows] = back_of(text_own, unit_ref[...], scale_col_ref[...]).T

    next_unit, next_scale = unit_scaled(dot_nn(visit, head_ref[...]))
    text_next = next_unit.astype(jnp.bfloat16)
    text_next_ref[...] = text_next
    weight_on = weight_turned(text_next, image_low_ref[...], -1.0, temper, offset)
    weight_on_ref[...] = weight_on
    weight_fn = weight_turned(text_next, image_far, -1.0, temper, offset)
    weight_fn_ref[...] = weight_fn
    text_part = dot_nn(weight_on, image_low_ref[...]) + dot_nn(weight_fn, image_far)
    part_ref[...] = text_part.astype(jnp.bfloat16)
    turned_ref[:, rows:] = back_of(text_part, next_unit, next_scale).T
    sorted_ref[...] = dot_nn(visit, spread_ref[...]).astype(jnp.bfloat16)

    pieces = NX * NYL
    share = turned_ref.shape[0] // (pieces * NC)
    for out_ref, core in ((mine_ref, core_ref[0]), (other_ref, 1 - core_ref[0])):
        starts = [pl.multiple_of((g * NC + core) * share, 8) for g in range(pieces)]
        cols = [turned_ref[pl.ds(start, share), :] for start in starts]
        out_ref[...] = jnp.concatenate(cols, axis=0).astype(jnp.bfloat16)


def in_vmem(kernel, scalars, arrays, shapes, macs, name, scratch=()):
    return pl.pallas_call(
        kernel,
        in_specs=[SMEM] * len(scalars) + [VMEM] * len(arrays),
        out_specs=[VMEM] * len(shapes),
        out_shape=[jax.ShapeDtypeStruct(*shape) for shape in shapes],
        scratch_shapes=scratch,
        compiler_params=pltpu.CompilerParams(vmem_limit_bytes=12 << 20),
        cost_estimate=pl.CostEstimate(flops=2 * macs, bytes_accessed=8 << 20, transcendentals=0),
        name=name,
    )(*scalars, *arrays)


def in_tiles(block):
    rows, cols = block.shape
    whole, left = cols // LANES, cols % LANES
    high = tail_rows(rows)
    tail = block[:, whole * LANES :]
    blank = jnp.zeros((2 * high - rows, left), block.dtype)
    tail = jnp.concatenate([tail[:high], jnp.concatenate([tail[high:], blank], axis=0)], axis=1)
    tiles = [block[:, t * LANES : (t + 1) * LANES] for t in range(whole)]
    return jnp.concatenate(tiles + [tail], axis=0)


def from_tiles(tiles, rows, cols):
    whole, left = cols // LANES, cols % LANES
    high = tail_rows(rows)
    tail = tiles[whole * rows :]
    tail = jnp.concatenate([tail[:, :left], tail[: rows - high, left : 2 * left]], axis=0)
    parts = [tiles[t * rows : (t + 1) * rows] for t in range(whole)]
    return jnp.concatenate(parts + [tail], axis=1)


def tail_rows(rows):
    return -(-rows // 2 // 8) * 8


def product_kernel(back_ref, feat_ref, visit_ref, *rest):
    out_ref = rest[-1]
    rows = feat_ref.shape[0]
    share = back_ref.shape[0] // (NX * NYL)
    used = back_ref.shape[0] * NC // NYH
    half = feat_ref.shape[1] // NYH
    for yh in range(NYH):
        lanes = slice(yh * half, (yh + 1) * half)
        total = dot_nn(back_ref[:, :rows], feat_ref[:, lanes])
        total += dot_nn(back_ref[:, rows:], visit_ref[:, lanes])
        for part in range(NX * NYL):
            peer = (part // NYL * NYH + yh) * NYL + part % NYL
            cut = in_tiles(total[part * share : (part + 1) * share, :used])
            if len(rest) > 1:
                cut += rest[0][peer].astype(jnp.float32)
            out_ref[peer] = cut.astype(jnp.bfloat16)


def head_product(back, feat, visit, *added):
    cols, rows = back.shape
    width = feat.shape[1]
    parts = NX * NYL
    share, used = cols // parts, cols * NC // NYH
    shape = (parts * NYH, used // LANES * share + tail_rows(share), LANES)
    return pl.pallas_call(
        product_kernel,
        in_specs=[VMEM] * (3 + len(added)),
        out_specs=VMEM,
        out_shape=jax.ShapeDtypeStruct(shape, jnp.bfloat16),
        compiler_params=LIMIT,
        cost_estimate=pl.CostEstimate(flops=2 * cols * rows * width, bytes_accessed=4 << 20, transcendentals=0),
        name="head_product",
    )(back, feat, visit, *added)


def pack_kernel(parts_ref, out_ref):
    slots, high, _ = out_ref.shape
    share, used = 3 * high, 3 * high * N_DX // NYH
    total = from_tiles(jnp.sum(parts_ref[...].astype(jnp.float32), axis=0), share, used)
    wide = total.shape[1] // slots
    blank = jnp.zeros((high, LANES - total.shape[0] // high * wide), jnp.float32)
    for z in range(slots):
        piece = total[:, z * wide : (z + 1) * wide]
        pieces = [piece[g * high : (g + 1) * high] for g in range(total.shape[0] // high)]
        out_ref[z] = jnp.concatenate(pieces + [blank], axis=1).astype(jnp.bfloat16)


def summed_and_packed(parts, share):
    return pl.pallas_call(
        pack_kernel,
        in_specs=[VMEM],
        out_specs=VMEM,
        out_shape=jax.ShapeDtypeStruct((NZ, share // 3, LANES), jnp.bfloat16),
        compiler_params=LIMIT,
        name="sum_x_y",
    )(parts)


def unpack_kernel(parts_ref, out_ref):
    total = jnp.sum(parts_ref[...].astype(jnp.float32), axis=0)
    wide, share = out_ref.shape
    high = total.shape[0]
    pieces = [total[:, g * wide : (g + 1) * wide] for g in range(share // high)]
    piece = jnp.concatenate(pieces, axis=0)
    piece = jnp.concatenate([piece, jnp.zeros((share, LANES - wide), jnp.float32)], axis=1)
    piece = jnp.concatenate([piece, jnp.zeros((LANES - share, LANES), jnp.float32)], axis=0)
    out_ref[...] = piece.T[:wide, :share]


def summed_over_z(parts, wide, share):
    return pl.pallas_call(
        unpack_kernel,
        in_specs=[VMEM],
        out_specs=VMEM,
        out_shape=jax.ShapeDtypeStruct((wide, share), jnp.float32),
        compiler_params=LIMIT,
        name="sum_z",
    )(parts)


def text_back_kernel(own_ref, home_ref, unit_ref, scale_col_ref, out_ref):
    text_sum = own_ref[...] + home_ref[...].astype(jnp.float32)
    out_ref[...] = back_of(text_sum, unit_ref[...], scale_col_ref[...]).astype(jnp.bfloat16)


def grad_image_kernel(own_ref, home_ref, image_ref, out_ref):
    image_sum = own_ref[...] + home_ref[...].astype(jnp.float32)
    image_unit, scale = unit_scaled(image_ref[...].astype(jnp.float32))
    out_ref[...] = back_of(image_sum, image_unit, scale)


def by_rows(kernel, arrays, dtype, flops, name):
    rows, width = arrays[0].shape
    tile = rows // 2
    return pl.pallas_call(
        kernel,
        grid=(rows // tile,),
        in_specs=[pl.BlockSpec((tile, array.shape[1]), lambda i: (i, 0)) for array in arrays],
        out_specs=pl.BlockSpec((tile, width), lambda i: (i, 0)),
        out_shape=jax.ShapeDtypeStruct((rows, width), dtype),
        compiler_params=LIMIT,
        cost_estimate=pl.CostEstimate(flops=flops, bytes_accessed=4 << 20, transcendentals=0),
        name=name,
    )(*arrays)


def local(image_emb, text_feat, text_head, log_scale, bias):
    rows, width = image_emb.shape
    wide = width // N_DY
    share = width // N_DX
    temper = jnp.exp(log_scale[0])
    offset = bias[0]
    scales = jnp.stack([temper, offset])
    core = (lax.axis_index("dx") % NC).astype(jnp.int32).reshape(1)

    low, high = jnp.bfloat16, jnp.float32

    text_first_here = core[0] == 0
    early = shifted(jnp.where(text_first_here, text_feat, image_emb), 1, -2)
    late = shifted(jnp.where(text_first_here, image_emb, text_feat), -2, 1)

    half = -(-width // NYH // LANES) * LANES
    place = np.arange(width)
    target = place // wide % NYH * half + place // (wide * NYH) * wide + place % wide
    target = jnp.asarray(target.reshape(width, 1), jnp.int32)
    block, square, column = (rows, width), (rows, rows), (rows, 1)
    sort = (rows, NYH * half)
    own = in_vmem(
        own_kernel,
        [scales],
        [text_feat, text_head, image_emb, target],
        [((width, NYH * half), low), (sort, low), (block, high), (column, high)]
        + [(block, low), (block, low), (square, low), (block, high)],
        rows * width * (width + 2 * rows + NYH * half),
        "own_blocks",
    )
    spread, feat_sorted, text_unit, text_scale, text_low, image_low, weight_own, text_first = own
    out = in_vmem(
        arrive_kernel,
        [core, scales],
        [early, late, text_head, spread, image_low, text_low, text_unit, text_scale, text_first],
        [(block, low), (block, low), (square, low), (square, low), (square, low), (block, high)]
        + [(block, low), (sort, low)]
        + [((width // NC, 2 * rows), low)] * 2,
        rows * width * (width + 6 * rows + NYH * half),
        "arrived",
        [pltpu.VMEM((width, 2 * rows), jnp.float32)],
    )
    image_far, text_next, weight_far, weight_on, weight_fn, text_own, text_part = out[:7]
    visit_sorted, back_mine, back_other = out[7:]

    head_other = head_product(back_other, feat_sorted, visit_sorted)
    head_in = lax.ppermute(head_other, "dx", [(p, p ^ 1) for p in range(N_DX)])
    text_part, _ = lax.optimization_barrier((text_part, head_other))
    text_home = shifted(text_part, -1, -1)
    head_part = head_product(back_mine, feat_sorted, visit_sorted, head_in)
    groups = [
        [
            ((x * NYL + yl) * NC + c) * N_DY + z * NYH + yh
            for x in range(NX)
            for yh in range(NYH)
            for yl in range(NYL)
        ]
        for c in range(NC)
        for z in range(NZ)
    ]
    late = (weight_own, weight_far, weight_on, weight_fn, text_own, head_part)
    weight_own, weight_far, weight_on, weight_fn, text_own, _ = lax.optimization_barrier(late)
    head_part = lax.all_to_all(head_part, ("dx", "dy"), 0, 0, axis_index_groups=groups, tiled=True)
    head_part = summed_and_packed(head_part, share)

    text_back = by_rows(
        text_back_kernel, [text_own, text_home, text_unit, text_scale], low, 2 * 10**10, "text_back"
    )
    image_part = dot_tn(weight_far, text_low) + dot_tn(weight_fn, text_next)
    image_home = shifted(image_part.astype(jnp.bfloat16), 2, 2)
    image_own = dot_tn(weight_own, text_low) + dot_tn(weight_on, text_next)

    late = (image_own, text_back, image_emb, head_part)
    image_own, text_back, image_emb, head_part = lax.optimization_barrier(late)
    groups = [[z * NYH + yh for z in range(NZ)] for yh in range(NYH)]
    head_part = lax.all_to_all(head_part, "dy", 0, 0, axis_index_groups=groups, tiled=True)
    grad_head = summed_over_z(head_part, wide, share)
    grad_image = by_rows(
        grad_image_kernel, [image_own, image_home, image_emb], high, 8 * rows * width, "grad_image"
    )
    grad_feat = dot_nt(text_back, text_head)
    return (grad_image, grad_feat, grad_head)


def solution(mesh):
    return jax.shard_map(
        local,
        mesh=mesh,
        in_specs=(P(("dx", "dy"), None), P(("dx", "dy"), None), P(), P(), P()),
        out_specs=(P(("dx", "dy"), None), P(("dx", "dy"), None), P("dy", "dx")),
        check_vma=False,
    )
```
